32 devices in a mesh: section: 2 (over core), dp: 4 (over z), tp: 4 (over y, x).
Axes of the slice: x: 2, y: 2, z: 4, core: 2. Of those that a mesh axis runs over, the one named last changes fastest.
Arguments:
- section_in: float32 [2, 1536, 640], P('section', ('dp', 'tp')), may hold values from -6 to 6
- seq_lengths: int32 [12], P('dp'), may hold values from 0 to 384, as said below
- attn_norm: float32 [2, 640], P('section'), may hold values from 0.25 to 1.75
- q_norm: float32 [2, 256], P('section'), may hold values from 0.55 to 1.45
- k_norm: float32 [2, 256], P('section'), may hold values from 0.55 to 1.45
- w_query: bfloat16 [2, 640, 1024], P('section', None, 'tp'), may hold values from -0.25 to 0.25
- w_key: bfloat16 [2, 640, 256], P('section', None, 'tp'), may hold values from -0.25 to 0.25
- w_value: bfloat16 [2, 640, 256], P('section', None, 'tp'), may hold values from -0.25 to 0.25
- w_out: bfloat16 [2, 1024, 640], P('section', 'tp'), may hold values from -0.1875 to 0.1875
- post_attn_norm: float32 [2, 640], P('section'), may hold values from 0.25 to 1.75
- ff_norm: float32 [2, 640], P('section'), may hold values from 0.25 to 1.75
- w_gate: bfloat16 [2, 640, 2048], P('section', None, 'tp'), may hold values from -0.25 to 0.25
- w_up: bfloat16 [2, 640, 2048], P('section', None, 'tp'), may hold values from -0.25 to 0.25
- w_down: bfloat16 [2, 2048, 640], P('section', 'tp'), may hold values from -0.125 to 0.125
- post_ff_norm: float32 [2, 640], P('section'), may hold values from 0.25 to 1.75
Outputs:
- section_out: float32 [2, 1536, 640], P('section', ('dp', 'tp'))
- attn_norm_grad: float32 [2, 640], P('section')
- q_norm_grad: float32 [2, 256], P('section')
- k_norm_grad: float32 [2, 256], P('section')
- w_query_grad: float32 [2, 640, 1024], P('section', None, 'tp')
- w_key_grad: float32 [2, 640, 256], P('section', None, 'tp')
- w_value_grad: float32 [2, 640, 256], P('section', None, 'tp')
- w_out_grad: float32 [2, 1024, 640], P('section', 'tp')
- post_attn_norm_grad: float32 [2, 640], P('section')
- ff_norm_grad: float32 [2, 640], P('section')
- w_gate_grad: float32 [2, 640, 2048], P('section', None, 'tp')
- w_up_grad: float32 [2, 640, 2048], P('section', None, 'tp')
- w_down_grad: float32 [2, 2048, 640], P('section', 'tp')
- post_ff_norm_grad: float32 [2, 640], P('section')
The draws below stay inside these ranges and needn't reach their ends.
Inputs may be any that keep to these rules, and one draw needn't show every extreme that they name: `seq_lengths`: in each group of 3 slots, the lengths rounded up to multiples of 128 add up to at most 384; some slot has length exactly 384.
All inputs are finite; a program needn't handle non-finite values.
Results may differ from the reference program's by a relative error of at most 0.025.
Values may be sent and summed in bfloat16 or wider, within the bound.
A program may use at most 128 MiB of HBM per device.

```python
import jax
import jax.numpy as jnp
from jax import lax

D = 640
HEADS = 4
HD = 256
FF = 2048
WINDOW = 512
BLOCK = 128
QBLOCK = 1024
TOK_DEV = 384
SEQ_LIM = 384
SEQ_DEV = 3
TOKENS = 1536
SEQS = 12
N_DP = 4


def gain_table(key):
    return 1.0 + 0.15 * jnp.clip(jax.random.normal(key, (2, HD), jnp.float32), -3.0, 3.0)


def draw_q_norm(key, part):
    return gain_table(jax.random.fold_in(key, 11))


def draw_k_norm(key, part):
    return gain_table(jax.random.fold_in(key, 23))


def draw_seq_lengths(key, part):
    group_count = SEQS // SEQ_DEV
    most_blocks = SEQ_LIM // BLOCK
    buffer_blocks = TOK_DEV // BLOCK
    base_key = jax.random.fold_in(key, 37)
    key_wanted, key_trim, key_full = jax.random.split(base_key, 3)
    wanted = jax.random.randint(key_wanted, (group_count, SEQ_DEV), 0, most_blocks + 1)
    full_group = jax.random.randint(key_full, (), 0, group_count)
    group_ids = jnp.arange(group_count)[:, None]
    slot_ids = jnp.arange(SEQ_DEV)[None, :]
    full_cell = (group_ids == full_group) & (slot_ids == 0)
    wanted = jnp.where(full_cell, most_blocks, wanted)
    used_before = jnp.cumsum(wanted, axis=1) - wanted
    granted = jnp.clip(jnp.minimum(wanted, buffer_blocks - used_before), 0, most_blocks)
    trimmed = jax.random.randint(key_trim, (group_count, SEQ_DEV), 0, BLOCK)
    lengths = jnp.where(granted > 0, granted * BLOCK - trimmed, 0)
    lengths = jnp.where(full_cell, SEQ_LIM, lengths)
    return lengths.reshape(-1).astype(jnp.int32)


def steps_of(stream_key, dims, cuts, low, largest):
    def one(axis_at, shards_of):
        heights = jax.random.uniform(jax.random.fold_in(jax.random.fold_in(stream_key, 6), axis_at), (shards_of,), jnp.float32, low / len(cuts), largest / len(cuts))
        return jnp.repeat(jnp.exp(heights), dims[axis_at] // shards_of).reshape((-1,) + (1,) * (len(dims) - axis_at - 1))

    factor_of = one(*cuts[0])
    for cut in cuts[1:]:
        factor_of = factor_of * one(*cut)
    return factor_of


def bell_draw(rng, extent, scale, most, shards=(), kind=jnp.bfloat16):
    loudness = steps_of(rng, extent, shards, -0.22, 0.18) if shards else 1.0
    entries = jax.random.normal(rng, extent, jnp.float32) * scale * loudness
    return jnp.minimum(jnp.maximum(entries, -most), most).astype(kind)


def setup_inputs(seed: int = 0) -> dict:
    keys = jax.random.split(jax.random.key(seed), 16)
    return {
        "section_in": bell_draw(keys[0], (2, TOKENS, D), 1.0, 6.0, ((0, 2), (1, 16)), jnp.float32),
        "seq_lengths": draw_seq_lengths(jax.random.fold_in(keys[15], 71), 0),
        "attn_norm": jnp.clip(1.0 + 0.15 * jax.random.normal(keys[2], (2, D), jnp.float32), 0.25, 1.75),
        "q_norm": draw_q_norm(jax.random.fold_in(keys[15], 71), 0),
        "k_norm": draw_k_norm(jax.random.fold_in(keys[15], 71), 0),
        "w_query": bell_draw(keys[5], (2, D, HEADS * HD), D ** -0.5, 0.25, ((0, 2), (2, 4))),
        "w_key": bell_draw(keys[6], (2, D, HD), D ** -0.5, 0.25, ((0, 2), (2, 4))),
        "w_value": bell_draw(keys[7], (2, D, HD), D ** -0.5, 0.25, ((0, 2), (2, 4))),
        "w_out": bell_draw(keys[8], (2, HEADS * HD, D), (HEADS * HD) ** -0.5, 0.1875, ((0, 2), (1, 4))),
        "post_attn_norm": jnp.clip(1.0 + 0.15 * jax.random.normal(keys[9], (2, D), jnp.float32), 0.25, 1.75),
        "ff_norm": jnp.clip(1.0 + 0.15 * jax.random.normal(keys[10], (2, D), jnp.float32), 0.25, 1.75),
        "w_gate": bell_draw(keys[11], (2, D, FF), D ** -0.5, 0.25, ((0, 2), (2, 4))),
        "w_up": bell_draw(keys[12], (2, D, FF), D ** -0.5, 0.25, ((0, 2), (2, 4))),
        "w_down": bell_draw(keys[13], (2, FF, D), FF ** -0.5, 0.125, ((0, 2), (1, 4))),
        "post_ff_norm": jnp.clip(1.0 + 0.15 * jax.random.normal(keys[14], (2, D), jnp.float32), 0.25, 1.75),
    }


EPSILON = 1e-06

def norm_stats(values):
    inverse = lax.rsqrt(lax.optimization_barrier(jnp.mean(values * values, axis=-1, keepdims=True)) + EPSILON)
    return (values * inverse, inverse)

def norm_back(normed, inverse, norm_gain, upstream):
    scaled = upstream * norm_gain
    result = inverse * (scaled - normed * lax.optimization_barrier(jnp.mean(scaled * normed, axis=-1, keepdims=True)))
    gain_grad = lax.optimization_barrier(jnp.sum((upstream * normed).reshape(-1, normed.shape[-1]), axis=0))
    return (result, gain_grad)

def rotate(values, cos_table, sin_table):
    half_width = values.shape[-1] // 2
    leading = values[..., :half_width]
    trailing = values[..., half_width:]
    return jnp.concatenate([leading * cos_table - trailing * sin_table, trailing * cos_table + leading * sin_table], axis=-1)

def rotate_back(upstream, cos_table, sin_table):
    half_width = upstream.shape[-1] // 2
    leading = upstream[..., :half_width]
    trailing = upstream[..., half_width:]
    return jnp.concatenate([leading * cos_table + trailing * sin_table, trailing * cos_table - leading * sin_table], axis=-1)

def layout(lengths, row_count):
    slot_count = lengths.shape[0]
    lengths = lengths.astype(jnp.int32)
    padded = (lengths + (BLOCK - 1)) // BLOCK * BLOCK
    seq_ends = jnp.cumsum(padded).astype(jnp.int32)
    offsets = jnp.arange(row_count, dtype=jnp.int32)
    segment = lax.optimization_barrier(jnp.sum((offsets[:, None] >= seq_ends[None, :]).astype(jnp.int32), axis=1)).astype(jnp.int32)
    seq_starts = jnp.concatenate([jnp.zeros((1,), jnp.int32), seq_ends])
    extended = jnp.concatenate([lengths, jnp.zeros((1,), jnp.int32)])
    chosen = segment[:, None] == jnp.arange(slot_count + 1, dtype=jnp.int32)[None, :]
    seq_start = lax.optimization_barrier(jnp.sum(jnp.where(chosen, seq_starts[None, :], 0), axis=1)).astype(jnp.int32)
    seq_length = lax.optimization_barrier(jnp.sum(jnp.where(chosen, extended[None, :], 0), axis=1)).astype(jnp.int32)
    position = offsets - seq_start
    return (segment, position, position < seq_length)

def tables(position, rope_base, head_width):
    half_width = head_width // 2
    exponent = jnp.arange(half_width, dtype=jnp.float32) * (2.0 / head_width)
    frequency = jnp.power(rope_base, -exponent)
    angles = position.astype(jnp.float32)[:, None] * frequency[None, :]
    return (jnp.cos(angles), jnp.sin(angles))

def allowed(seg_query, pos_query, seg_key, pos_key, window):
    distance = pos_query[:, None] - pos_key[None, :]
    return (seg_query[:, None] == seg_key[None, :]) & (distance >= 0) & (distance < window)

def key_pad(key_rows, values, segment, position, padding):
    if padding == 0:
        return (key_rows, values, segment, position)
    blank_rows = jnp.zeros((padding, key_rows.shape[1]), key_rows.dtype)
    return (jnp.concatenate([blank_rows, key_rows]), jnp.concatenate([blank_rows, values]), jnp.concatenate([jnp.full((padding,), -1, jnp.int32), segment]), jnp.concatenate([jnp.zeros((padding,), jnp.int32), position]))

def block_plan(row_count):
    block_rows = min(QBLOCK, row_count)
    blocks = row_count // block_rows
    padding = block_rows if blocks > 1 else 0
    return (block_rows, blocks, padding)

def attend(queries, key_rows, values, segment, position, window):
    row_count, head_count, head_width = queries.shape
    block_rows, blocks, padding = block_plan(row_count)
    key_span = block_rows + padding
    score_scale = head_width ** (-0.5)
    padded_keys, padded_values, key_segment, key_position = key_pad(key_rows, values, segment, position, padding)

    def one_block(block_index):
        row_start = block_index * block_rows
        query_block = lax.dynamic_slice_in_dim(queries, row_start, block_rows, 0)
        key_block = lax.dynamic_slice_in_dim(padded_keys, row_start, key_span, 0)
        value_block = lax.dynamic_slice_in_dim(padded_values, row_start, key_span, 0)
        visible = allowed(lax.dynamic_slice_in_dim(segment, row_start, block_rows, 0), lax.dynamic_slice_in_dim(position, row_start, block_rows, 0), lax.dynamic_slice_in_dim(key_segment, row_start, key_span, 0), lax.dynamic_slice_in_dim(key_position, row_start, key_span, 0), window)
        scores = score_scale * jnp.einsum('qhd,kd->hqk', query_block.astype(jnp.float32), key_block.astype(jnp.float32))
        scores = jnp.where(visible[None], scores, -1e+30)
        highest = lax.optimization_barrier(jnp.max(scores, axis=-1, keepdims=True))
        weights = jnp.where(visible[None], jnp.exp(scores - highest), 0.0)
        totals = lax.optimization_barrier(jnp.sum(weights, axis=-1, keepdims=True))
        probability = (weights / totals).astype(jnp.bfloat16)
        output = jnp.einsum('hqk,kd->qhd', probability.astype(jnp.float32), value_block.astype(jnp.float32)).astype(jnp.bfloat16)
        log_total = jnp.transpose((highest + jnp.log(totals))[..., 0])
        return (output, log_total)
    outputs, log_totals = lax.map(one_block, jnp.arange(blocks, dtype=jnp.int32))
    return (outputs.reshape(row_count, head_count, head_width), log_totals.reshape(row_count, head_count))

def attend_back(queries, key_rows, values, segment, position, window, attended, log_totals, attended_grad):
    row_count, head_count, head_width = queries.shape
    block_rows, blocks, padding = block_plan(row_count)
    key_span = block_rows + padding
    score_scale = head_width ** (-0.5)
    padded_keys, padded_values, key_segment, key_position = key_pad(key_rows, values, segment, position, padding)

    def one_step(running, block_index):
        key_acc, value_acc = running
        row_start = block_index * block_rows
        query_block = lax.dynamic_slice_in_dim(queries, row_start, block_rows, 0)
        key_block = lax.dynamic_slice_in_dim(padded_keys, row_start, key_span, 0)
        value_block = lax.dynamic_slice_in_dim(padded_values, row_start, key_span, 0)
        visible = allowed(lax.dynamic_slice_in_dim(segment, row_start, block_rows, 0), lax.dynamic_slice_in_dim(position, row_start, block_rows, 0), lax.dynamic_slice_in_dim(key_segment, row_start, key_span, 0), lax.dynamic_slice_in_dim(key_position, row_start, key_span, 0), window)
        scores = score_scale * jnp.einsum('qhd,kd->hqk', query_block.astype(jnp.float32), key_block.astype(jnp.float32))
        scores = jnp.where(visible[None], scores, -1e+30)
        log_block = jnp.transpose(lax.dynamic_slice_in_dim(log_totals, row_start, block_rows, 0))[:, :, None]
        probability = jnp.where(visible[None], jnp.exp(scores - log_block), 0.0)
        low_prob = probability.astype(jnp.bfloat16)
        grad_block = lax.dynamic_slice_in_dim(attended_grad, row_start, block_rows, 0).astype(jnp.float32)
        att_block = lax.dynamic_slice_in_dim(attended, row_start, block_rows, 0).astype(jnp.float32)
        prob_grad = jnp.einsum('qhd,kd->hqk', grad_block, value_block.astype(jnp.float32))
        delta = jnp.transpose(lax.optimization_barrier(jnp.sum(grad_block * att_block, axis=-1)))[:, :, None]
        score_grad = (probability * (prob_grad - delta)).astype(jnp.bfloat16).astype(jnp.float32)
        query_grad = score_scale * jnp.einsum('hqk,kd->qhd', score_grad, key_block.astype(jnp.float32))
        key_grad = score_scale * jnp.einsum('hqk,qhd->kd', score_grad, query_block.astype(jnp.float32))
        value_grad = jnp.einsum('hqk,qhd->kd', low_prob.astype(jnp.float32), grad_block)
        key_acc = lax.dynamic_update_slice_in_dim(key_acc, lax.dynamic_slice_in_dim(key_acc, row_start, key_span, 0) + key_grad, row_start, 0)
        value_acc = lax.dynamic_update_slice_in_dim(value_acc, lax.dynamic_slice_in_dim(value_acc, row_start, key_span, 0) + value_grad, row_start, 0)
        return ((key_acc, value_acc), query_grad)
    blank_acc = jnp.zeros((row_count + padding, head_width), jnp.float32)
    (key_acc, value_acc), query_grads = lax.scan(one_step, (blank_acc, blank_acc), jnp.arange(blocks, dtype=jnp.int32))
    return (query_grads.reshape(row_count, head_count, head_width), key_acc[padding:], value_acc[padding:])

def gelu_tanh(values):
    return jax.nn.gelu(values, approximate=True)

def layer_forward(hidden_in, params, context):
    attn_gain, query_gain, key_gain, w_query, w_key, w_value, w_out, post_attn_gain, ff_gain, w_gate, w_up, w_down, post_ff_gain = params
    segment, position, cos_table, sin_table, window = context
    row_count = hidden_in.shape[0]
    head_width = query_gain.shape[0]
    head_count = w_query.shape[1] // head_width
    normed_in, inverse_in = norm_stats(hidden_in)
    attn_input = (normed_in * attn_gain).astype(jnp.bfloat16)
    queries = jnp.dot(attn_input, w_query, preferred_element_type=jnp.float32).reshape(row_count, head_count, head_width)
    keys_raw = jnp.dot(attn_input, w_key, preferred_element_type=jnp.float32).astype(jnp.bfloat16)
    values = jnp.dot(attn_input, w_value, preferred_element_type=jnp.float32).astype(jnp.bfloat16)
    query_normed, query_inverse = norm_stats(queries)
    query_rot = rotate(query_normed * query_gain, cos_table[:, None], sin_table[:, None]).astype(jnp.bfloat16)
    key_normed, key_inverse = norm_stats(keys_raw.astype(jnp.float32))
    key_rot = rotate(key_normed * key_gain, cos_table, sin_table).astype(jnp.bfloat16)
    attended, log_totals = attend(query_rot, key_rot, values, segment, position, window)
    attn_flat = attended.reshape(row_count, head_count * head_width)
    attn_sum = jnp.dot(attn_flat, w_out, preferred_element_type=jnp.float32)
    out_normed, out_inverse = norm_stats(attn_sum)
    middle = hidden_in + out_normed * post_attn_gain
    mid_normed, mid_inverse = norm_stats(middle)
    ff_input = (mid_normed * ff_gain).astype(jnp.bfloat16)
    gate_pre = jnp.dot(ff_input, w_gate, preferred_element_type=jnp.float32)
    upward = jnp.dot(ff_input, w_up, preferred_element_type=jnp.float32)
    active = gelu_tanh(gate_pre)
    hidden = (active * upward).astype(jnp.bfloat16)
    ff_sum = jnp.dot(hidden, w_down, preferred_element_type=jnp.float32)
    ff_normed, ff_inverse = norm_stats(ff_sum)
    result = middle + ff_normed * post_ff_gain
    stored = dict(normed_in=normed_in, inverse_in=inverse_in, attn_input=attn_input, query_normed=query_normed, query_inverse=query_inverse, key_normed=key_normed, key_inverse=key_inverse, query_rot=query_rot, key_rot=key_rot, values=values, attended=attended, log_totals=log_totals, attn_flat=attn_flat, out_normed=out_normed, out_inverse=out_inverse, mid_normed=mid_normed, mid_inverse=mid_inverse, ff_input=ff_input, gate_pre=gate_pre, upward=upward, active=active, hidden=hidden, ff_normed=ff_normed, ff_inverse=ff_inverse)
    return (result, stored)

def layer_backward(params, stored, upstream, context):
    attn_gain, query_gain, key_gain, w_query, w_key, w_value, w_out, post_attn_gain, ff_gain, w_gate, w_up, w_down, post_ff_gain = params
    segment, position, cos_table, sin_table, window = context
    row_count = upstream.shape[0]
    head_width = query_gain.shape[0]
    head_count = w_query.shape[1] // head_width
    ff_grad, post_ff_grad = norm_back(stored['ff_normed'], stored['ff_inverse'], post_ff_gain, upstream)
    ff_cot = ff_grad.astype(jnp.bfloat16)
    hidden_grad = jnp.dot(ff_cot, w_down.T, preferred_element_type=jnp.float32)
    down_grad = jnp.dot(stored['hidden'].T, ff_cot, preferred_element_type=jnp.float32)
    gelu_out, slope = jax.vjp(gelu_tanh, stored['gate_pre'])
    gate_low = slope(hidden_grad * stored['upward'])[0].astype(jnp.bfloat16)
    up_low = (hidden_grad * stored['active']).astype(jnp.bfloat16)
    gate_wgrad = jnp.dot(stored['ff_input'].T, gate_low, preferred_element_type=jnp.float32)
    up_wgrad = jnp.dot(stored['ff_input'].T, up_low, preferred_element_type=jnp.float32)
    ff_input_grad = jnp.dot(gate_low, w_gate.T, preferred_element_type=jnp.float32) + jnp.dot(up_low, w_up.T, preferred_element_type=jnp.float32)
    mid_back, ff_gain_grad = norm_back(stored['mid_normed'], stored['mid_inverse'], ff_gain, ff_input_grad)
    middle_grad = upstream + mid_back
    attn_grad, post_attn_grad = norm_back(stored['out_normed'], stored['out_inverse'], post_attn_gain, middle_grad)
    attn_cot = attn_grad.astype(jnp.bfloat16)
    out_wgrad = jnp.dot(stored['attn_flat'].T, attn_cot, preferred_element_type=jnp.float32)
    attended_grad = jnp.dot(attn_cot, w_out.T, preferred_element_type=jnp.float32).astype(jnp.bfloat16).reshape(row_count, head_count, head_width)
    query_rgrad, key_rgrad, value_grad = attend_back(stored['query_rot'], stored['key_rot'], stored['values'], segment, position, window, stored['attended'], stored['log_totals'], attended_grad)
    query_back, query_gain_grad = norm_back(stored['query_normed'], stored['query_inverse'], query_gain, rotate_back(query_rgrad, cos_table[:, None], sin_table[:, None]))
    key_back, key_gain_grad = norm_back(stored['key_normed'], stored['key_inverse'], key_gain, rotate_back(key_rgrad, cos_table, sin_table))
    query_low = query_back.astype(jnp.bfloat16).reshape(row_count, head_count * head_width)
    key_low = key_back.astype(jnp.bfloat16)
    value_low = value_grad.astype(jnp.bfloat16)
    attn_input = stored['attn_input']
    query_wgrad = jnp.dot(attn_input.T, query_low, preferred_element_type=jnp.float32)
    key_wgrad = jnp.dot(attn_input.T, key_low, preferred_element_type=jnp.float32)
    value_wgrad = jnp.dot(attn_input.T, value_low, preferred_element_type=jnp.float32)
    input_grad = jnp.dot(query_low, w_query.T, preferred_element_type=jnp.float32) + jnp.dot(key_low, w_key.T, preferred_element_type=jnp.float32) + jnp.dot(value_low, w_value.T, preferred_element_type=jnp.float32)
    in_back, attn_gain_grad = norm_back(stored['normed_in'], stored['inverse_in'], attn_gain, input_grad)
    grads = (attn_gain_grad, query_gain_grad, key_gain_grad, query_wgrad, key_wgrad, value_wgrad, out_wgrad, post_attn_grad, ff_gain_grad, gate_wgrad, up_wgrad, down_grad, post_ff_grad)
    return (grads, middle_grad + in_back)

def reference(section_in, seq_lengths, attn_norm, q_norm, k_norm, w_query, w_key, w_value, w_out, post_attn_norm, ff_norm, w_gate, w_up, w_down, post_ff_norm):
    weights = (attn_norm, q_norm, k_norm, w_query, w_key, w_value, w_out, post_attn_norm, ff_norm, w_gate, w_up, w_down, post_ff_norm)
    first_params = tuple((weight[0] for weight in weights))
    second_params = tuple((weight[1] for weight in weights))
    inputs = section_in[0].reshape(N_DP, TOK_DEV, D)
    cotangent = section_in[1].reshape(N_DP, TOK_DEV, D)
    lengths = seq_lengths.reshape(N_DP, SEQ_DEV).astype(jnp.int32)
    blank_grads = tuple((jnp.zeros(weight.shape[1:], jnp.float32) for weight in weights))

    def one_group(running, buffer_item):
        first_grads, second_grads = running
        hidden_in, upstream, group_lengths = buffer_item
        segment, position, valid_rows = layout(group_lengths, TOK_DEV)
        cos_one, sin_one = tables(position, 10000.0, HD)
        cos_two, sin_two = tables(position, 1000000.0, HD)
        first_ctx = (segment, position, cos_one, sin_one, WINDOW)
        second_ctx = (segment, position, cos_two, sin_two, TOK_DEV + 1)
        middle_out, first_stored = layer_forward(hidden_in, first_params, first_ctx)
        final_out, second_stored = layer_forward(middle_out, second_params, second_ctx)
        masked = upstream * valid_rows.astype(jnp.float32)[:, None]
        grads_two, middle_grad = layer_backward(second_params, second_stored, masked, second_ctx)
        grads_one, input_grad = layer_backward(first_params, first_stored, middle_grad, first_ctx)
        first_grads = jax.tree.map(lambda former, latter: former + latter, first_grads, grads_one)
        second_grads = jax.tree.map(lambda former, latter: former + latter, second_grads, grads_two)
        return ((first_grads, second_grads), (final_out, input_grad))
    (first_grads, second_grads), (final_out, input_grad) = lax.scan(one_group, (blank_grads, blank_grads), (inputs, cotangent, lengths))
    section_out = jnp.stack([input_grad.reshape(TOKENS, D), final_out.reshape(TOKENS, D)])
    stacked = tuple((jnp.stack([former, latter]) for former, latter in zip(first_grads, second_grads)))
    return (section_out, stacked[0], stacked[1], stacked[2], stacked[3], stacked[4], stacked[5], stacked[6], stacked[7], stacked[8], stacked[9], stacked[10], stacked[11], stacked[12])
```

```python
import functools

import jax
import jax.numpy as jnp
from jax import lax
from jax.experimental import pallas as pl
from jax.experimental.pallas import tpu as pltpu
from jax.sharding import PartitionSpec as P

WINDOW = 512
BLOCK = 128
EPSILON = 1e-06
F32 = jnp.float32
BF16 = jnp.bfloat16
MESH = pl.DeviceIdType.MESH


def layout(lengths, row_count):
    slot_count = lengths.shape[0]
    padded = (lengths + (BLOCK - 1)) // BLOCK * BLOCK
    slots = jnp.arange(slot_count)
    seq_ends = jnp.sum(jnp.where(slots[:, None] <= slots[None, :], padded[:, None], 0), axis=0)
    offsets = jnp.arange(row_count, dtype=jnp.int32)
    segment = jnp.sum((offsets[:, None] >= seq_ends[None, :]).astype(jnp.int32), axis=1)
    seq_starts = jnp.concatenate([jnp.zeros((1,), jnp.int32), seq_ends])
    extended = jnp.concatenate([lengths, jnp.zeros((1,), jnp.int32)])
    chosen = segment[:, None] == jnp.arange(slot_count + 1, dtype=jnp.int32)[None, :]
    seq_start = jnp.sum(jnp.where(chosen, seq_starts[None, :], 0), axis=1)
    seq_length = jnp.sum(jnp.where(chosen, extended[None, :], 0), axis=1)
    position = offsets - seq_start
    return (segment, position, position < seq_length)


def tables(position, rope_base, head_width):
    half_width = head_width // 2
    exponent = jnp.arange(half_width, dtype=jnp.float32) * (2.0 / head_width)
    frequency = jnp.power(rope_base, -exponent)
    angles = position.astype(jnp.float32)[:, None] * frequency[None, :]
    return (jnp.cos(angles), jnp.sin(angles))


def stats(values):
    inverse = lax.rsqrt(jnp.mean(values * values, axis=-1, keepdims=True) + EPSILON)
    return values * inverse, inverse


def norm_back(normed, inverse, gain, upstream):
    scaled = upstream * gain
    result = inverse * (scaled - normed * jnp.mean(scaled * normed, axis=-1, keepdims=True))
    return result, jnp.sum(upstream * normed, axis=0, keepdims=True)


def rotate(values, cos, sin):
    half = values.shape[-1] // 2
    lead, trail = values[:, :half], values[:, half:]
    return jnp.concatenate([lead * cos - trail * sin, trail * cos + lead * sin], axis=-1)


def rotate_back(values, cos, sin):
    half = values.shape[-1] // 2
    lead, trail = values[:, :half], values[:, half:]
    return jnp.concatenate([lead * cos + trail * sin, trail * cos - lead * sin], axis=-1)


def dot(x, y):
    return jnp.dot(x, y, preferred_element_type=F32)


def dot_nt(x, y):
    return lax.dot_general(x, y, (((1,), (1,)), ((), ())), preferred_element_type=F32)


def dot_tn(x, y):
    return lax.dot_general(x, y, (((0,), (0,)), ((), ())), preferred_element_type=F32)


def layer_kernel(
    tp,
    x_ref, valid_ref, bias_ref, cos_ref, sin_ref,
    g_attn, g_q, g_k, wq, wk, wv, wo, g_pa, g_ff, wg, wu, wd, g_pf,
    sect_out, gains_out, dwq, dwk, dwv, dwo, dwg, dwu, dwd,
    wkv_all, wkf, wvf, hbuf, xbuf, sbuf,
    a_all, b_all, df_all, do_all,
    o_send, o_recv, f_send, f_recv, db_send, db_recv, da_send, da_recv, kv_send, kv_recv,
    qn_s, qi_s, kn_s, ki_s, qr_s, kr_s, v_s, p_s, att_s,
    gate_s, up_s, act_s, hid_s, slope_s, dgate_s, dup_s, dq_s, dk_s, dv_s, own_s, dmid_s,
    send_sem, recv_sem, x_send_sem, x_recv_sem,
):
    sec = lax.axis_index("section")
    me = lax.axis_index("tp")
    other = 1 - sec
    rows, width = x_ref.shape
    cols = wk.shape[1]
    scale = g_q.shape[1] ** (-0.5)
    peers = [lax.rem(me + k, tp) for k in range(tp)]
    mine = pl.ds(pl.multiple_of(me * rows, 16), rows)

    barrier = pltpu.get_barrier_semaphore()
    for k in range(1, tp):
        pl.semaphore_signal(barrier, inc=1, device_id={"tp": peers[k]}, device_id_type=MESH)
    pl.semaphore_signal(barrier, inc=1, device_id={"section": other}, device_id_type=MESH)
    pl.semaphore_wait(barrier, tp)

    pending = []

    def copy(ex, k, src, dst):
        return pltpu.make_async_remote_copy(
            src_ref=src, dst_ref=dst,
            send_sem=send_sem.at[ex, k - 1], recv_sem=recv_sem.at[ex, k - 1],
            device_id={"tp": peers[k]}, device_id_type=MESH,
        )

    def spread(ex, buf, where):
        copies = [copy(ex, k, buf.at[where], buf.at[where]) for k in range(1, tp)]
        for c in copies:
            c.start()
        pending.extend(copies)
        return copies

    def arrived(copies):
        for c in copies:
            c.wait_recv()

    def scatter(ex, send, recv, make):
        copies = []
        for k in range(1, tp):
            at = pl.ds(pl.multiple_of(peers[k] * rows, 16), rows)
            send[k - 1] = make(at).astype(BF16)
            c = copy(ex, k, send.at[k - 1], recv.at[k - 1])
            c.start()
            copies.append(c)
        own_s[...] = make(mine)
        pending.extend(copies)
        return copies

    def total(copies, recv):
        acc = own_s[...]
        for k in range(1, tp):
            copies[k - 1].wait_recv()
            acc = acc + recv[k - 1].astype(F32)
        return acc

    wkv_all[me] = jnp.concatenate([wk[...], wv[...]], axis=1)
    kvw = spread(0, wkv_all, me)

    cross = pltpu.make_async_remote_copy(
        src_ref=sbuf, dst_ref=xbuf, send_sem=x_send_sem, recv_sem=x_recv_sem,
        device_id={"section": other}, device_id_type=MESH,
    )

    arrived(kvw)
    for j in range(tp):
        block = wkv_all[j]
        wkf[:, j * cols:(j + 1) * cols] = block[:, :cols]
        wvf[:, j * cols:(j + 1) * cols] = block[:, cols:]

    @pl.when(sec == 0)
    def _():
        hbuf[...] = x_ref[...]

    @pl.when(sec == 1)
    def _():
        cross.wait_recv()
        hbuf[...] = xbuf[...]

    h = hbuf[...]
    n_in, i_in = stats(h)
    a_all[mine] = (n_in * g_attn[...]).astype(BF16)
    arrived(spread(1, a_all, mine))
    a = a_all[...]
    cos, sin = cos_ref[...], sin_ref[...]
    qn, qi = stats(dot(a, wq[...]))
    qn_s[...] = qn
    qi_s[...] = qi
    qr_s[...] = rotate(qn * g_q[...], cos, sin).astype(BF16)
    kn, ki = stats(dot(a, wkf[...]).astype(BF16).astype(F32))
    kn_s[...] = kn
    ki_s[...] = ki
    kr_s[...] = rotate(kn * g_k[...], cos, sin).astype(BF16)
    v_s[...] = dot(a, wvf[...]).astype(BF16)
    s = dot_nt(qr_s[...], kr_s[...]) * scale + bias_ref[...]
    e = jnp.exp(s - jnp.max(s, axis=-1, keepdims=True))
    p = e / jnp.sum(e, axis=-1, keepdims=True)
    p_s[...] = p
    att_s[...] = dot(p.astype(BF16), v_s[...]).astype(BF16)
    o_copies = scatter(2, o_send, o_recv, lambda at: dot(att_s[at], wo[...]))
    n_o, i_o = stats(total(o_copies, o_recv))
    mid = hbuf[...] + n_o * g_pa[...]
    n_mid, i_mid = stats(mid)
    b_all[mine] = (n_mid * g_ff[...]).astype(BF16)
    arrived(spread(3, b_all, mine))
    gate = dot(b_all[...], wg[...])
    up = dot(b_all[...], wu[...])
    gate_s[...] = gate
    up_s[...] = up
    c0 = 0.7978845608028654
    t = jnp.tanh(c0 * (gate + 0.044715 * gate * gate * gate))
    act = 0.5 * gate * (1.0 + t)
    act_s[...] = act
    hid_s[...] = (act * up).astype(BF16)
    slope_s[...] = t
    f_copies = scatter(4, f_send, f_recv, lambda at: dot(hid_s[at], wd[...]))
    gate = gate_s[...]
    t = slope_s[...]
    slope = 0.5 * (1.0 + t) + 0.5 * c0 * gate * (1.0 - t * t) * (1.0 + 3 * 0.044715 * gate * gate)
    slope_s[...] = slope * up_s[...]
    n_f, i_f = stats(total(f_copies, f_recv))
    out = mid + n_f * g_pf[...]

    @pl.when(sec == 0)
    def _():
        sbuf[...] = out
        cross.start()
        cross.wait_recv()
        hbuf[...] = xbuf[...]

    @pl.when(sec == 1)
    def _():
        sect_out[...] = out
        hbuf[...] = x_ref[...] * valid_ref[...]

    up_g = hbuf[...]
    df, dg_pf = norm_back(n_f, i_f, g_pf[...], up_g)
    df_all[mine] = df.astype(BF16)
    arrived(spread(5, df_all, mine))
    dhid = dot_nt(df_all[...], wd[...])
    dgate_s[...] = (dhid * slope_s[...]).astype(BF16)
    dup_s[...] = (dhid * act_s[...]).astype(BF16)
    db_copies = scatter(
        6, db_send, db_recv,
        lambda at: dot_nt(dgate_s[at], wg[...]) + dot_nt(dup_s[at], wu[...]),
    )
    dwd[...] = dot_tn(hid_s[...], df_all[...]).astype(dwd.dtype)
    db = total(db_copies, db_recv)
    mid_back, dg_ff = norm_back(n_mid, i_mid, g_ff[...], db)
    dmid = hbuf[...] + mid_back
    dmid_s[...] = dmid
    do, dg_pa = norm_back(n_o, i_o, g_pa[...], dmid)
    do_all[mine] = do.astype(BF16)
    do_copies = spread(7, do_all, mine)
    dwg[...] = dot_tn(b_all[...], dgate_s[...]).astype(dwg.dtype)
    arrived(do_copies)
    datt_f = dot_nt(do_all[...], wo[...])
    datt = datt_f.astype(BF16)
    delta = jnp.sum(datt.astype(F32) * att_s[...].astype(F32), axis=-1, keepdims=True)
    p = p_s[...]
    ds = (p * (dot_nt(datt, v_s[...]) - delta)).astype(BF16)
    dqr = dot(ds, kr_s[...]) * scale
    dkr = dot_tn(ds, qr_s[...]) * scale
    dv = dot_tn(p.astype(BF16), datt)
    dq, dg_q = norm_back(qn_s[...], qi_s[...], g_q[...], rotate_back(dqr, cos, sin))
    dk, dg_k = norm_back(kn_s[...], ki_s[...], g_k[...], rotate_back(dkr, cos, sin))
    dq_s[...] = dq.astype(BF16)
    dk_s[...] = dk.astype(BF16)
    dv_s[...] = dv.astype(BF16)
    da_copies = scatter(
        8, da_send, da_recv,
        lambda at: dot_nt(dq_s[at], wq[...]) + dot_nt(dk_s[at], wkf[...]) + dot_nt(dv_s[at], wvf[...]),
    )
    for j in range(tp):
        kv_send[j] = jnp.concatenate(
            [dk_s[:, j * cols:(j + 1) * cols], dv_s[:, j * cols:(j + 1) * cols]], axis=1
        )
    kv_copies = []
    for k in range(1, tp):
        c = copy(9, k, kv_send.at[peers[k]], kv_recv.at[k - 1])
        c.start()
        kv_copies.append(c)
    pending.extend(kv_copies)
    dwq[...] = dot_tn(a_all[...], dq_s[...]).astype(dwq.dtype)
    da = total(da_copies, da_recv)
    in_back, dg_attn = norm_back(n_in, i_in, g_attn[...], da)
    dh = dmid_s[...] + in_back

    @pl.when(sec == 1)
    def _():
        sbuf[...] = dh
        cross.start()

    @pl.when(sec == 0)
    def _():
        sect_out[...] = dh

    dwu[...] = dot_tn(b_all[...], dup_s[...]).astype(dwu.dtype)
    dwo[...] = dot_tn(att_s[...], do_all[...]).astype(dwo.dtype)
    dkv = kv_send[me].astype(F32)
    for k in range(1, tp):
        kv_copies[k - 1].wait_recv()
        dkv = dkv + kv_recv[k - 1].astype(F32)
    dwkv = dot_tn(a_all[...], dkv.astype(BF16))
    dwk[...] = dwkv[:, :cols].astype(dwk.dtype)
    dwv[...] = dwkv[:, cols:].astype(dwv.dtype)
    zero = jnp.zeros((1, width - dg_q.shape[1] - dg_k.shape[1]), F32)
    last = jnp.concatenate([dg_q, dg_k, zero], axis=1)
    gains_out[...] = jnp.concatenate(
        [dg_attn, dg_pa, dg_ff, dg_pf, last, jnp.zeros((3, width), F32)], axis=0
    )
    for c in pending:
        c.wait_send()
    cross.wait_send()


def local(
    section_in, seq_lengths, attn_norm, q_norm, k_norm, w_query, w_key, w_value, w_out,
    post_attn_norm, ff_norm, w_gate, w_up, w_down, post_ff_norm,
):
    first = lax.axis_index("section") == 0
    tp = lax.axis_size("tp")
    tp_index = lax.axis_index("tp")
    x = section_in[0]
    rows, width = x.shape
    n = rows * tp
    hd = q_norm.shape[-1]
    ff = w_gate.shape[2]
    cols = w_key.shape[2]
    segment, position, valid_rows = layout(seq_lengths, n)
    valid = lax.dynamic_slice_in_dim(valid_rows, tp_index * rows, rows, 0).astype(F32)[:, None]
    window = jnp.where(first, WINDOW, n + 1)
    rope_base = jnp.where(first, 10000.0, 1000000.0).astype(F32)
    cos, sin = tables(position, rope_base, hd)
    distance = position[:, None] - position[None, :]
    visible = (segment[:, None] == segment[None, :]) & (distance >= 0) & (distance < window)
    bias = jnp.where(visible, 0.0, -1e30).astype(F32)
    gt = BF16
    sds = jax.ShapeDtypeStruct
    vm = pltpu.VMEM
    rs = lambda: vm((tp - 1, rows, width), BF16)
    ag = lambda: vm((n, width), BF16)
    outs = pl.pallas_call(
        functools.partial(layer_kernel, tp),
        out_shape=[
            sds((rows, width), F32), sds((8, width), F32),
            sds((width, hd), gt), sds((width, cols), gt), sds((width, cols), gt),
            sds((hd, width), gt), sds((width, ff), gt), sds((width, ff), gt), sds((ff, width), gt),
        ],
        in_specs=[pl.BlockSpec(memory_space=pltpu.VMEM)] * 18,
        out_specs=[pl.BlockSpec(memory_space=pltpu.VMEM)] * 9,
        scratch_shapes=[
            vm((tp, width, 2 * cols), BF16), vm((width, hd), BF16), vm((width, hd), BF16),
            vm((rows, width), F32), vm((rows, width), F32), vm((rows, width), F32),
            ag(), ag(), ag(), ag(),
            rs(), rs(), rs(), rs(), rs(), rs(), rs(), rs(),
            vm((tp, n, 2 * cols), BF16), vm((tp - 1, n, 2 * cols), BF16),
            vm((n, hd), F32), vm((n, 1), F32), vm((n, hd), F32), vm((n, 1), F32),
            vm((n, hd), BF16), vm((n, hd), BF16), vm((n, hd), BF16), vm((n, n), F32), vm((n, hd), BF16),
            vm((n, ff), F32), vm((n, ff), F32), vm((n, ff), F32), vm((n, ff), BF16), vm((n, ff), F32),
            vm((n, ff), BF16), vm((n, ff), BF16), vm((n, hd), BF16), vm((n, hd), BF16), vm((n, hd), BF16),
            vm((rows, width), F32), vm((rows, width), F32),
            pltpu.SemaphoreType.DMA((10, tp - 1)), pltpu.SemaphoreType.DMA((10, tp - 1)),
            pltpu.SemaphoreType.DMA, pltpu.SemaphoreType.DMA,
        ],
        compiler_params=pltpu.CompilerParams(
            collective_id=0, has_side_effects=True, vmem_limit_bytes=56 * 1024 * 1024
        ),
    )(
        x, valid, bias, cos, sin, attn_norm, q_norm, k_norm, w_query[0], w_key[0], w_value[0],
        w_out[0], post_attn_norm, ff_norm, w_gate[0], w_up[0], w_down[0], post_ff_norm,
    )
    section_out, gains = outs[0], outs[1]
    gains = lax.psum(gains, ("dp", "tp"))
    mats = [m.astype(F32)[None] for m in lax.psum(tuple(outs[2:]), "dp")]
    row = lambda i: gains[i:i + 1]
    return (
        section_out[None], row(0), gains[4:5, :hd], gains[4:5, hd:2 * hd],
        mats[0], mats[1], mats[2], mats[3], row(1), row(2), mats[4], mats[5], mats[6], row(3),
    )


def solution(mesh):
    grid = P("section", None, "tp")
    down = P("section", "tp", None)
    gain = P("section", None)
    act = P("section", ("dp", "tp"), None)
    return jax.shard_map(
        local,
        mesh=mesh,
        in_specs=(
            act, P("dp"), gain, gain, gain, grid, grid, grid, down, gain, gain, grid, grid, down, gain,
        ),
        out_specs=(
            act, gain, gain, gain, grid, grid, grid, down, gain, gain, grid, grid, down, gain,
        ),
        check_vma=False,
    )
```

```python
import functools

import jax
import jax.numpy as jnp
from jax import lax
from jax.experimental import pallas as pl
from jax.experimental.pallas import tpu as pltpu
from jax.sharding import PartitionSpec as P

WINDOW = 512
BLOCK = 128
EPSILON = 1e-06
F32 = jnp.float32
BF16 = jnp.bfloat16
MESH = pl.DeviceIdType.MESH


def layout(lengths, row_count):
    slot_count = lengths.shape[0]
    padded = (lengths + (BLOCK - 1)) // BLOCK * BLOCK
    slots = jnp.arange(slot_count)
    seq_ends = jnp.sum(jnp.where(slots[:, None] <= slots[None, :], padded[:, None], 0), axis=0)
    offsets = jnp.arange(row_count, dtype=jnp.int32)
    segment = jnp.sum((offsets[:, None] >= seq_ends[None, :]).astype(jnp.int32), axis=1)
    seq_starts = jnp.concatenate([jnp.zeros((1,), jnp.int32), seq_ends])
    extended = jnp.concatenate([lengths, jnp.zeros((1,), jnp.int32)])
    chosen = segment[:, None] == jnp.arange(slot_count + 1, dtype=jnp.int32)[None, :]
    seq_start = jnp.sum(jnp.where(chosen, seq_starts[None, :], 0), axis=1)
    seq_length = jnp.sum(jnp.where(chosen, extended[None, :], 0), axis=1)
    position = offsets - seq_start
    return (segment, position, position < seq_length)


def tables(position, rope_base, head_width):
    half_width = head_width // 2
    exponent = jnp.arange(half_width, dtype=jnp.float32) * (2.0 / head_width)
    frequency = jnp.power(rope_base, -exponent)
    angles = position.astype(jnp.float32)[:, None] * frequency[None, :]
    return (jnp.cos(angles), jnp.sin(angles))


def stats(values):
    inverse = lax.rsqrt(jnp.mean(values * values, axis=-1, keepdims=True) + EPSILON)
    return values * inverse, inverse


def norm_back(normed, inverse, gain, upstream):
    scaled = upstream * gain
    result = inverse * (scaled - normed * jnp.mean(scaled * normed, axis=-1, keepdims=True))
    return result, jnp.sum(upstream * normed, axis=0, keepdims=True)


def rotate(values, cos, sin):
    half = values.shape[-1] // 2
    lead, trail = values[:, :half], values[:, half:]
    return jnp.concatenate([lead * cos - trail * sin, trail * cos + lead * sin], axis=-1)


def rotate_back(values, cos, sin):
    half = values.shape[-1] // 2
    lead, trail = values[:, :half], values[:, half:]
    return jnp.concatenate([lead * cos + trail * sin, trail * cos - lead * sin], axis=-1)


def dot(x, y):
    return jnp.dot(x, y, preferred_element_type=F32)


def dot_nt(x, y):
    return lax.dot_general(x, y, (((1,), (1,)), ((), ())), preferred_element_type=F32)


def dot_tn(x, y):
    return lax.dot_general(x, y, (((0,), (0,)), ((), ())), preferred_element_type=F32)


def layer_kernel(
    tp, dp, inside,
    x_ref, valid_ref, bias_ref, cos_ref, sin_ref,
    g_attn, g_q, g_k, wq, wk, wv, wo, g_pa, g_ff, wg, wu, wd, g_pf,
    sect_out, gains_out, dwq, dwk, dwv, dwo, dwg, dwu, dwd,
    wkv_all, wkf, wvf, hbuf, xbuf, sbuf,
    a_all, b_all, df_all, do_all,
    o_send, o_recv, f_send, f_recv, db_send, db_recv, da_send, da_recv, kv_send, kv_recv,
    qn_s, qi_s, kn_s, ki_s, qr_s, kr_s, v_s, p_s, att_s,
    gate_s, up_s, act_s, hid_s, slope_s, dgate_s, dup_s, dq_s, dk_s, dv_s, own_s, dmid_s,
    send_sem, recv_sem, x_send_sem, x_recv_sem, *dp_refs,
):
    sec = lax.axis_index("section")
    me = lax.axis_index("tp")
    other = 1 - sec
    rows, width = x_ref.shape
    cols = wk.shape[1]
    scale = g_q.shape[1] ** (-0.5)
    peers = [lax.rem(me + k, tp) for k in range(tp)]
    mine = pl.ds(pl.multiple_of(me * rows, 16), rows)

    barrier = pltpu.get_barrier_semaphore()
    for k in range(1, tp):
        pl.semaphore_signal(barrier, inc=1, device_id={"tp": peers[k]}, device_id_type=MESH)
    pl.semaphore_signal(barrier, inc=1, device_id={"section": other}, device_id_type=MESH)
    if inside:
        z = lax.axis_index("dp")
        for k in range(1, dp):
            pl.semaphore_signal(
                barrier, inc=1, device_id={"dp": lax.rem(z + k, dp)}, device_id_type=MESH
            )
    pl.semaphore_wait(barrier, tp + (dp - 1 if inside else 0))

    pending = []

    def copy(ex, k, src, dst):
        return pltpu.make_async_remote_copy(
            src_ref=src, dst_ref=dst,
            send_sem=send_sem.at[ex, k - 1], recv_sem=recv_sem.at[ex, k - 1],
            device_id={"tp": peers[k]}, device_id_type=MESH,
        )

    def spread(ex, buf, where):
        copies = [copy(ex, k, buf.at[where], buf.at[where]) for k in range(1, tp)]
        for c in copies:
            c.start()
        pending.extend(copies)
        return copies

    def arrived(copies):
        for c in copies:
            c.wait_recv()

    def scatter(ex, send, recv, make):
        copies = []
        for k in range(1, tp):
            at = pl.ds(pl.multiple_of(peers[k] * rows, 16), rows)
            send[k - 1] = make(at).astype(BF16)
            c = copy(ex, k, send.at[k - 1], recv.at[k - 1])
            c.start()
            copies.append(c)
        own_s[...] = make(mine)
        pending.extend(copies)
        return copies

    def total(copies, recv):
        acc = own_s[...]
        for k in range(1, tp):
            copies[k - 1].wait_recv()
            acc = acc + recv[k - 1].astype(F32)
        return acc

    if inside:
        dkv_s, gain_tp, gain_dp, d_send, d_recv, g_send, g_recv = dp_refs[-7:]
        low, high = lax.rem(z, 2), lax.rem(z // 2, 2)
        near, far = z + 1 - 2 * low, z + 2 - 4 * high
        grads = [dwd.at[0], dwg.at[0], dwu.at[0], dwo.at[0], dwq.at[0], dkv_s]
        live = {}

        def place(ref, start, size):
            return ref.at[pl.ds(pl.multiple_of(start, 16), size)]

        def move(i, step, src, dst, peer):
            c = pltpu.make_async_remote_copy(
                src_ref=src, dst_ref=dst, send_sem=d_send.at[i, step], recv_sem=d_recv.at[i, step],
                device_id={"dp": peer}, device_id_type=MESH,
            )
            c.start()
            pending.append(c)
            live[i] = c

        def advance(step, *which):
            for i in which:
                acc = grads[i]
                first_out, first_in, second_out, second_in, whole = dp_refs[5 * i:5 * i + 5]
                half, quarter = acc.shape[0] // 2, acc.shape[0] // 4
                own_half = low * half
                own_quarter = own_half + high * quarter
                if step > 0:
                    live[i].wait_recv()
                if step == 0:
                    first_out[...] = place(acc, (1 - low) * half, half)[...].astype(BF16)
                    move(i, 0, first_out, first_in, near)
                elif step == 1:
                    kept = place(acc, own_half, half)
                    kept[...] = kept[...] + first_in[...].astype(F32)
                    second_out[...] = place(acc, own_half + (1 - high) * quarter, quarter)[...].astype(BF16)
                    move(i, 1, second_out, second_in, far)
                elif step == 2:
                    done = place(whole, own_quarter, quarter)
                    done[...] = (place(acc, own_quarter, quarter)[...] + second_in[...].astype(F32)).astype(BF16)
                    move(i, 2, done, done, far)
                elif step == 3:
                    done = place(whole, own_half, half)
                    move(i, 3, done, done, near)
                elif i < 5:
                    acc[...] = whole[...].astype(F32)
                else:
                    dwk[0] = whole[:, :cols].astype(F32)
                    dwv[0] = whole[:, cols:].astype(F32)
    else:
        dkv_s = dp_refs[0]

        def advance(step, *which):
            pass

    wkv_all[me] = jnp.concatenate([wk[...], wv[...]], axis=1)
    kvw = spread(0, wkv_all, me)

    cross = pltpu.make_async_remote_copy(
        src_ref=sbuf, dst_ref=xbuf, send_sem=x_send_sem, recv_sem=x_recv_sem,
        device_id={"section": other}, device_id_type=MESH,
    )

    arrived(kvw)
    for j in range(tp):
        block = wkv_all[j]
        wkf[:, j * cols:(j + 1) * cols] = block[:, :cols]
        wvf[:, j * cols:(j + 1) * cols] = block[:, cols:]

    @pl.when(sec == 0)
    def _():
        hbuf[...] = x_ref[...]

    @pl.when(sec == 1)
    def _():
        cross.wait_recv()
        hbuf[...] = xbuf[...]

    h = hbuf[...]
    n_in, i_in = stats(h)
    a_all[mine] = (n_in * g_attn[...]).astype(BF16)
    arrived(spread(1, a_all, mine))
    a = a_all[...]
    cos, sin = cos_ref[...], sin_ref[...]
    qn, qi = stats(dot(a, wq[...]))
    qn_s[...] = qn
    qi_s[...] = qi
    qr_s[...] = rotate(qn * g_q[...], cos, sin).astype(BF16)
    kn, ki = stats(dot(a, wkf[...]).astype(BF16).astype(F32))
    kn_s[...] = kn
    ki_s[...] = ki
    kr_s[...] = rotate(kn * g_k[...], cos, sin).astype(BF16)
    v_s[...] = dot(a, wvf[...]).astype(BF16)
    s = dot_nt(qr_s[...], kr_s[...]) * scale + bias_ref[...]
    e = jnp.exp(s - jnp.max(s, axis=-1, keepdims=True))
    p = e / jnp.sum(e, axis=-1, keepdims=True)
    p_s[...] = p
    att_s[...] = dot(p.astype(BF16), v_s[...]).astype(BF16)
    o_copies = scatter(2, o_send, o_recv, lambda at: dot(att_s[at], wo[...]))
    n_o, i_o = stats(total(o_copies, o_recv))
    mid = hbuf[...] + n_o * g_pa[...]
    n_mid, i_mid = stats(mid)
    b_all[mine] = (n_mid * g_ff[...]).astype(BF16)
    arrived(spread(3, b_all, mine))
    gate = dot(b_all[...], wg[...])
    up = dot(b_all[...], wu[...])
    gate_s[...] = gate
    up_s[...] = up
    c0 = 0.7978845608028654
    t = jnp.tanh(c0 * (gate + 0.044715 * gate * gate * gate))
    act = 0.5 * gate * (1.0 + t)
    act_s[...] = act
    hid_s[...] = (act * up).astype(BF16)
    slope_s[...] = t
    f_copies = scatter(4, f_send, f_recv, lambda at: dot(hid_s[at], wd[...]))
    gate = gate_s[...]
    t = slope_s[...]
    slope = 0.5 * (1.0 + t) + 0.5 * c0 * gate * (1.0 - t * t) * (1.0 + 3 * 0.044715 * gate * gate)
    slope_s[...] = slope * up_s[...]
    n_f, i_f = stats(total(f_copies, f_recv))
    out = mid + n_f * g_pf[...]

    @pl.when(sec == 0)
    def _():
        sbuf[...] = out
        cross.start()
        cross.wait_recv()
        hbuf[...] = xbuf[...]

    @pl.when(sec == 1)
    def _():
        sect_out[...] = out
        hbuf[...] = x_ref[...] * valid_ref[...]

    up_g = hbuf[...]
    df, dg_pf = norm_back(n_f, i_f, g_pf[...], up_g)
    df_all[mine] = df.astype(BF16)
    arrived(spread(5, df_all, mine))
    dhid = dot_nt(df_all[...], wd[...])
    dgate_s[...] = (dhid * slope_s[...]).astype(BF16)
    dup_s[...] = (dhid * act_s[...]).astype(BF16)
    db_copies = scatter(
        6, db_send, db_recv,
        lambda at: dot_nt(dgate_s[at], wg[...]) + dot_nt(dup_s[at], wu[...]),
    )
    dwd[0] = dot_tn(hid_s[...], df_all[...])
    advance(0, 0)
    dwg[0] = dot_tn(b_all[...], dgate_s[...])
    advance(0, 1)
    dwu[0] = dot_tn(b_all[...], dup_s[...])
    advance(0, 2)
    db = total(db_copies, db_recv)
    mid_back, dg_ff = norm_back(n_mid, i_mid, g_ff[...], db)
    dmid = hbuf[...] + mid_back
    dmid_s[...] = dmid
    do, dg_pa = norm_back(n_o, i_o, g_pa[...], dmid)
    do_all[mine] = do.astype(BF16)
    do_copies = spread(7, do_all, mine)
    arrived(do_copies)
    datt_f = dot_nt(do_all[...], wo[...])
    datt = datt_f.astype(BF16)
    delta = jnp.sum(datt.astype(F32) * att_s[...].astype(F32), axis=-1, keepdims=True)
    p = p_s[...]
    ds = (p * (dot_nt(datt, v_s[...]) - delta)).astype(BF16)
    dqr = dot(ds, kr_s[...]) * scale
    dkr = dot_tn(ds, qr_s[...]) * scale
    dv = dot_tn(p.astype(BF16), datt)
    dq, dg_q = norm_back(qn_s[...], qi_s[...], g_q[...], rotate_back(dqr, cos, sin))
    dk, dg_k = norm_back(kn_s[...], ki_s[...], g_k[...], rotate_back(dkr, cos, sin))
    dq_s[...] = dq.astype(BF16)
    dk_s[...] = dk.astype(BF16)
    dv_s[...] = dv.astype(BF16)
    da_copies = scatter(
        8, da_send, da_recv,
        lambda at: dot_nt(dq_s[at], wq[...]) + dot_nt(dk_s[at], wkf[...]) + dot_nt(dv_s[at], wvf[...]),
    )
    for j in range(tp):
        kv_send[j] = jnp.concatenate(
            [dk_s[:, j * cols:(j + 1) * cols], dv_s[:, j * cols:(j + 1) * cols]], axis=1
        )
    kv_copies = []
    for k in range(1, tp):
        c = copy(9, k, kv_send.at[peers[k]], kv_recv.at[k - 1])
        c.start()
        kv_copies.append(c)
    pending.extend(kv_copies)
    dwo[0] = dot_tn(att_s[...], do_all[...])
    advance(0, 3)
    advance(1, 0, 1, 2)
    da = total(da_copies, da_recv)
    in_back, dg_attn = norm_back(n_in, i_in, g_attn[...], da)
    dh = dmid_s[...] + in_back

    @pl.when(sec == 1)
    def _():
        sbuf[...] = dh
        cross.start()

    @pl.when(sec == 0)
    def _():
        sect_out[...] = dh

    zero = jnp.zeros((1, width - dg_q.shape[1] - dg_k.shape[1]), F32)
    gains = jnp.concatenate(
        [dg_attn, dg_pa, dg_ff, dg_pf, jnp.concatenate([dg_q, dg_k, zero], axis=1),
         jnp.zeros((3, width), F32)], axis=0
    )
    gain_copies = []
    if inside:
        gain_tp[me] = gains
        for k in range(1, tp):
            c = pltpu.make_async_remote_copy(
                src_ref=gain_tp.at[me], dst_ref=gain_tp.at[me], send_sem=g_send.at[0, k - 1],
                recv_sem=g_recv.at[0, k - 1], device_id={"tp": peers[k]}, device_id_type=MESH,
            )
            c.start()
            gain_copies.append(c)
    else:
        gains_out[...] = gains
    dwq[0] = dot_tn(a_all[...], dq_s[...])
    advance(0, 4)
    dkv = kv_send[me].astype(F32)
    for k in range(1, tp):
        kv_copies[k - 1].wait_recv()
        dkv = dkv + kv_recv[k - 1].astype(F32)
    dkv_s[...] = dot_tn(a_all[...], dkv.astype(BF16))
    advance(0, 5)
    if inside:
        advance(2, 0, 1, 2)
        advance(1, 3)
        for c in gain_copies:
            c.wait_recv()
        gain_dp[z] = sum(gain_tp[j] for j in range(tp))
        more = []
        for k in range(1, dp):
            c = pltpu.make_async_remote_copy(
                src_ref=gain_dp.at[z], dst_ref=gain_dp.at[z], send_sem=g_send.at[1, k - 1],
                recv_sem=g_recv.at[1, k - 1], device_id={"dp": lax.rem(z + k, dp)},
                device_id_type=MESH,
            )
            c.start()
            more.append(c)
        pending.extend(gain_copies + more)
        advance(1, 4, 5)
        advance(3, 0, 1, 2)
        advance(2, 3, 4, 5)
        advance(3, 3, 4, 5)
        for c in more:
            c.wait_recv()
        gains_out[...] = sum(gain_dp[j] for j in range(dp))
        advance(4, 0, 1, 2, 3, 4, 5)
    else:
        dwk[0] = dkv_s[:, :cols]
        dwv[0] = dkv_s[:, cols:]
    for c in pending:
        c.wait_send()
    cross.wait_send()


def local(
    section_in, seq_lengths, attn_norm, q_norm, k_norm, w_query, w_key, w_value, w_out,
    post_attn_norm, ff_norm, w_gate, w_up, w_down, post_ff_norm,
):
    first = lax.axis_index("section") == 0
    tp = lax.axis_size("tp")
    tp_index = lax.axis_index("tp")
    x = section_in[0]
    rows, width = x.shape
    n = rows * tp
    hd = q_norm.shape[-1]
    ff = w_gate.shape[2]
    cols = w_key.shape[2]
    segment, position, valid_rows = layout(seq_lengths, n)
    valid = lax.dynamic_slice_in_dim(valid_rows, tp_index * rows, rows, 0).astype(F32)[:, None]
    window = jnp.where(first, WINDOW, n + 1)
    rope_base = jnp.where(first, 10000.0, 1000000.0).astype(F32)
    cos, sin = tables(position, rope_base, hd)
    distance = position[:, None] - position[None, :]
    visible = (segment[:, None] == segment[None, :]) & (distance >= 0) & (distance < window)
    bias = jnp.where(visible, 0.0, -1e30).astype(F32)
    dp = lax.axis_size("dp")
    inside = dp == 4 and width % 64 == 0 and hd % 64 == 0 and ff % 64 == 0
    sds = jax.ShapeDtypeStruct
    vm = pltpu.VMEM
    rs = lambda: vm((tp - 1, rows, width), BF16)
    ag = lambda: vm((n, width), BF16)
    across = [vm((width, 2 * cols), F32)]
    if inside:
        across = []
        for m, w in ((ff, width), (width, ff), (width, ff), (hd, width), (width, hd), (width, 2 * cols)):
            across += [vm((m // 2, w), BF16)] * 2 + [vm((m // 4, w), BF16)] * 2 + [vm((m, w), BF16)]
        sem = pltpu.SemaphoreType.DMA
        across += [
            vm((width, 2 * cols), F32), vm((tp, 8, width), F32), vm((dp, 8, width), F32),
            sem((6, 4)), sem((6, 4)), sem((2, max(tp, dp) - 1)), sem((2, max(tp, dp) - 1)),
        ]
    outs = pl.pallas_call(
        functools.partial(layer_kernel, tp, dp, inside),
        out_shape=[
            sds((rows, width), F32), sds((8, width), F32),
            sds((1, width, hd), F32), sds((1, width, cols), F32), sds((1, width, cols), F32),
            sds((1, hd, width), F32), sds((1, width, ff), F32), sds((1, width, ff), F32),
            sds((1, ff, width), F32),
        ],
        in_specs=[pl.BlockSpec(memory_space=pltpu.VMEM)] * 18,
        out_specs=[pl.BlockSpec(memory_space=pltpu.VMEM)] * 9,
        scratch_shapes=[
            vm((tp, width, 2 * cols), BF16), vm((width, hd), BF16), vm((width, hd), BF16),
            vm((rows, width), F32), vm((rows, width), F32), vm((rows, width), F32),
            ag(), ag(), ag(), ag(),
            rs(), rs(), rs(), rs(), rs(), rs(), rs(), rs(),
            vm((tp, n, 2 * cols), BF16), vm((tp - 1, n, 2 * cols), BF16),
            vm((n, hd), F32), vm((n, 1), F32), vm((n, hd), F32), vm((n, 1), F32),
            vm((n, hd), BF16), vm((n, hd), BF16), vm((n, hd), BF16), vm((n, n), F32), vm((n, hd), BF16),
            vm((n, ff), F32), vm((n, ff), F32), vm((n, ff), F32), vm((n, ff), BF16), vm((n, ff), F32),
            vm((n, ff), BF16), vm((n, ff), BF16), vm((n, hd), BF16), vm((n, hd), BF16), vm((n, hd), BF16),
            vm((rows, width), F32), vm((rows, width), F32),
            pltpu.SemaphoreType.DMA((10, tp - 1)), pltpu.SemaphoreType.DMA((10, tp - 1)),
            pltpu.SemaphoreType.DMA, pltpu.SemaphoreType.DMA,
        ] + across,
        compiler_params=pltpu.CompilerParams(
            collective_id=0, has_side_effects=True, vmem_limit_bytes=56 * 1024 * 1024
        ),
    )(
        x, valid, bias, cos, sin, attn_norm, q_norm, k_norm, w_query[0], w_key[0], w_value[0],
        w_out[0], post_attn_norm, ff_norm, w_gate[0], w_up[0], w_down[0], post_ff_norm,
    )
    section_out, gains = outs[0], outs[1]
    mats = list(outs[2:])
    if not inside:
        gains = lax.psum(gains, ("dp", "tp"))
        mats = [m.astype(F32) for m in lax.psum(tuple(m.astype(BF16) for m in mats), "dp")]
    row = lambda i: gains[i:i + 1]
    return (
        section_out[None], row(0), gains[4:5, :hd], gains[4:5, hd:2 * hd],
        mats[0], mats[1], mats[2], mats[3], row(1), row(2), mats[4], mats[5], mats[6], row(3),
    )


def solution(mesh):
    grid = P("section", None, "tp")
    down = P("section", "tp", None)
    gain = P("section", None)
    act = P("section", ("dp", "tp"), None)
    return jax.shard_map(
        local,
        mesh=mesh,
        in_specs=(
            act, P("dp"), gain, gain, gain, grid, grid, grid, down, gain, gain, grid, grid, down, gain,
        ),
        out_specs=(
            act, gain, gain, gain, grid, grid, grid, down, gain, gain, grid, grid, down, gain,
        ),
        check_vma=False,
    )
```

```python
import functools

import jax
import jax.numpy as jnp
from jax import lax
from jax.experimental import pallas as pl
from jax.experimental.pallas import tpu as pltpu
from jax.sharding import PartitionSpec as P

WINDOW = 512
BLOCK = 128
EPSILON = 1e-06
F32 = jnp.float32
BF16 = jnp.bfloat16
MESH = pl.DeviceIdType.MESH


def layout(lengths, row_count):
    slot_count = lengths.shape[0]
    padded = (lengths + (BLOCK - 1)) // BLOCK * BLOCK
    slots = jnp.arange(slot_count)
    seq_ends = jnp.sum(jnp.where(slots[:, None] <= slots[None, :], padded[:, None], 0), axis=0)
    offsets = jnp.arange(row_count, dtype=jnp.int32)
    segment = jnp.sum((offsets[:, None] >= seq_ends[None, :]).astype(jnp.int32), axis=1)
    seq_starts = jnp.concatenate([jnp.zeros((1,), jnp.int32), seq_ends])
    extended = jnp.concatenate([lengths, jnp.zeros((1,), jnp.int32)])
    chosen = segment[:, None] == jnp.arange(slot_count + 1, dtype=jnp.int32)[None, :]
    seq_start = jnp.sum(jnp.where(chosen, seq_starts[None, :], 0), axis=1)
    seq_length = jnp.sum(jnp.where(chosen, extended[None, :], 0), axis=1)
    position = offsets - seq_start
    return (segment, position, position < seq_length)


def tables(position, rope_base, head_width):
    half_width = head_width // 2
    exponent = jnp.arange(half_width, dtype=jnp.float32) * (2.0 / head_width)
    frequency = jnp.power(rope_base, -exponent)
    angles = position.astype(jnp.float32)[:, None] * frequency[None, :]
    return (jnp.cos(angles), jnp.sin(angles))


def stats(values):
    inverse = lax.rsqrt(jnp.mean(values * values, axis=-1, keepdims=True) + EPSILON)
    return values * inverse, inverse


def norm_back(normed, inverse, gain, upstream):
    scaled = upstream * gain
    result = inverse * (scaled - normed * jnp.mean(scaled * normed, axis=-1, keepdims=True))
    return result, jnp.sum(upstream * normed, axis=0, keepdims=True)


def rotate(values, cos, sin):
    half = values.shape[-1] // 2
    lead, trail = values[:, :half], values[:, half:]
    return jnp.concatenate([lead * cos - trail * sin, trail * cos + lead * sin], axis=-1)


def rotate_back(values, cos, sin):
    half = values.shape[-1] // 2
    lead, trail = values[:, :half], values[:, half:]
    return jnp.concatenate([lead * cos + trail * sin, trail * cos - lead * sin], axis=-1)


def dot(x, y):
    return jnp.dot(x, y, preferred_element_type=F32)


def dot_nt(x, y):
    return lax.dot_general(x, y, (((1,), (1,)), ((), ())), preferred_element_type=F32)


def dot_tn(x, y):
    return lax.dot_general(x, y, (((0,), (0,)), ((), ())), preferred_element_type=F32)


def layer_kernel(
    tp, dp, inside,
    x_ref, valid_ref, bias_ref, cos_ref, sin_ref,
    g_attn, g_q, g_k, wq, wk, wv, wo, g_pa, g_ff, wg, wu, wd, g_pf,
    sect_out, gains_out, owq, owk, owv, owo, owg, owu, owd,
    dwq, dwo, dwg, dwu, dwd,
    wkf, wvf, hbuf, xbuf, sbuf,
    a_all, b_all, df_all, do_all,
    o_send, o_recv, f_send, f_recv, db_send, db_recv, da_send, da_recv, kv_send, kv_recv,
    qn_s, qi_s, kn_s, ki_s, qr_s, kr_s, v_s, p_s, att_s,
    gate_s, up_s, act_s, hid_s, slope_s, dgate_s, dup_s, dq_s, dk_s, dv_s, own_s, dmid_s,
    send_sem, recv_sem, x_send_sem, x_recv_sem, *dp_refs,
):
    sec = lax.axis_index("section")
    me = lax.axis_index("tp")
    other = 1 - sec
    rows, width = x_ref.shape
    cols = wk.shape[0]
    scale = g_q.shape[1] ** (-0.5)
    if tp == 4:
        first = me + 1 - 2 * lax.rem(me, 2)
        second = me + 2 - 4 * lax.rem(me // 2, 2)
        peers = [me, 3 - me, first, second]
    else:
        peers = [lax.rem(me + k, tp) for k in range(tp)]
    mine = pl.ds(pl.multiple_of(me * rows, 16), rows)

    barrier = pltpu.get_barrier_semaphore()
    for k in range(1, tp):
        pl.semaphore_signal(barrier, inc=1, device_id={"tp": peers[k]}, device_id_type=MESH)
    pl.semaphore_signal(barrier, inc=1, device_id={"section": other}, device_id_type=MESH)
    if inside:
        z = lax.axis_index("dp")
        for k in range(1, dp):
            pl.semaphore_signal(
                barrier, inc=1, device_id={"dp": lax.rem(z + k, dp)}, device_id_type=MESH
            )
    pl.semaphore_wait(barrier, tp + (dp - 1 if inside else 0))

    pending = []

    def copy(ex, k, src, dst):
        return pltpu.make_async_remote_copy(
            src_ref=src, dst_ref=dst,
            send_sem=send_sem.at[ex, k - 1], recv_sem=recv_sem.at[ex, k - 1],
            device_id={"tp": peers[k]}, device_id_type=MESH,
        )

    def spread(ex, buf, where):
        copies = [copy(ex, k, buf.at[where], buf.at[where]) for k in range(1, tp)]
        for c in copies:
            c.start()
        pending.extend(copies)
        return copies

    def arrived(copies):
        for c in copies:
            c.wait_recv()

    def scatter(ex, send, recv, make):
        copies = []
        for k in range(1, tp):
            at = pl.ds(pl.multiple_of(peers[k] * rows, 16), rows)
            send[k - 1] = make(at).astype(BF16)
            c = copy(ex, k, send.at[k - 1], recv.at[k - 1])
            c.start()
            copies.append(c)
        own_s[...] = make(mine)
        pending.extend(copies)
        return copies

    def total(copies, recv):
        acc = own_s[...]
        for k in range(1, tp):
            copies[k - 1].wait_recv()
            acc = acc + recv[k - 1].astype(F32)
        return acc

    if inside:
        dkv_s, gain_tp, gain_dp, d_send, d_recv, g_send, g_recv = dp_refs[-7:]
        middle = jnp.logical_and(z >= 1, z <= 2)
        edge = jnp.logical_not(middle)
        near = z + 1 - 2 * lax.rem(z, 2)
        across = 3 - z
        side = lax.rem(z + 1, 2)
        grads = [dwd.at[0], dwg.at[0], dwu.at[0], dwo.at[0], dwq.at[0], dkv_s]
        finals = [owd, owg, owu, owo, owq]

        def place(ref, start, size):
            return ref.at[pl.ds(pl.multiple_of(start, 16), size)]

        def move(i, step, src, dst, peer):
            return pltpu.make_async_remote_copy(
                src_ref=src, dst_ref=dst, send_sem=d_send.at[i, step], recv_sem=d_recv.at[i, step],
                device_id={"dp": peer}, device_id_type=MESH,
            )

        plan = []
        for i in range(6):
            all_out, all_in, half_out, half_in, whole = dp_refs[5 * i:5 * i + 5]
            half = whole.shape[0] // 2
            done = place(whole, side * half, half)
            plan.append((
                move(i, 0, all_out, all_in, near), move(i, 1, half_out, half_in, across),
                move(i, 2, done, done, across), move(i, 3, whole, whole, near),
            ))

        def advance(step, *which):
            for i in which:
                acc = grads[i]
                all_out, all_in, half_out, half_in, whole = dp_refs[5 * i:5 * i + 5]
                half = whole.shape[0] // 2
                c = plan[i]

                @pl.when(edge)
                def _():
                    if step == 0:
                        all_out[...] = acc[...].astype(BF16)
                        c[0].start()
                    elif step == 4:
                        c[3].wait_recv()

                @pl.when(middle)
                def _():
                    if step == 1:
                        c[0].wait_recv()
                        acc[...] = acc[...] + all_in[...].astype(F32)
                        half_out[...] = place(acc, (1 - side) * half, half)[...].astype(BF16)
                        c[1].start()
                    elif step == 2:
                        c[1].wait_recv()
                        place(whole, side * half, half)[...] = (
                            place(acc, side * half, half)[...] + half_in[...].astype(F32)
                        ).astype(BF16)
                        c[2].start()
                    elif step == 3:
                        c[2].wait_recv()
                        c[3].start()

                if step == 4:
                    if i < 5:
                        finals[i][0] = whole[...]
                    else:
                        owk[0] = whole[:cols]
                        owv[0] = whole[cols:]
    else:
        dkv_s = dp_refs[0]

        def advance(step, *which):
            pass

    own_cols = pl.ds(pl.multiple_of(me * cols, 16), cols)
    wkf[own_cols] = wk[...]
    wvf[own_cols] = wv[...]

    cross = pltpu.make_async_remote_copy(
        src_ref=sbuf, dst_ref=xbuf, send_sem=x_send_sem, recv_sem=x_recv_sem,
        device_id={"section": other}, device_id_type=MESH,
    )

    @pl.when(sec == 0)
    def _():
        hbuf[...] = x_ref[...]

    @pl.when(sec == 1)
    def _():
        cross.wait_recv()
        hbuf[...] = xbuf[...]

    h = hbuf[...]
    n_in, i_in = stats(h)
    a_all[mine] = (n_in * g_attn[...]).astype(BF16)
    a_copies = spread(1, a_all, mine)
    kvw = spread(0, wkf, own_cols) + spread(10, wvf, own_cols)
    arrived(a_copies)
    a = a_all[...]
    cos, sin = cos_ref[...], sin_ref[...]
    qn, qi = stats(dot(a, wq[...]))
    qn_s[...] = qn
    qi_s[...] = qi
    qr_s[...] = rotate(qn * g_q[...], cos, sin).astype(BF16)
    arrived(kvw)
    kn, ki = stats(dot_nt(a, wkf[...]).astype(BF16).astype(F32))
    kn_s[...] = kn
    ki_s[...] = ki
    kr_s[...] = rotate(kn * g_k[...], cos, sin).astype(BF16)
    v_s[...] = dot_nt(a, wvf[...]).astype(BF16)
    s = dot_nt(qr_s[...], kr_s[...]) * scale + bias_ref[...]
    e = jnp.exp(s - jnp.max(s, axis=-1, keepdims=True))
    p = e / jnp.sum(e, axis=-1, keepdims=True)
    p_s[...] = p
    att_s[...] = dot(p.astype(BF16), v_s[...]).astype(BF16)
    o_copies = scatter(2, o_send, o_recv, lambda at: dot(att_s[at], wo[...]))
    n_o, i_o = stats(total(o_copies, o_recv))
    mid = hbuf[...] + n_o * g_pa[...]
    n_mid, i_mid = stats(mid)
    b_all[mine] = (n_mid * g_ff[...]).astype(BF16)
    arrived(spread(3, b_all, mine))
    gate = dot(b_all[...], wg[...])
    up = dot(b_all[...], wu[...])
    gate_s[...] = gate
    up_s[...] = up
    c0 = 0.7978845608028654
    t = jnp.tanh(c0 * (gate + 0.044715 * gate * gate * gate))
    act = 0.5 * gate * (1.0 + t)
    act_s[...] = act
    hid_s[...] = (act * up).astype(BF16)
    slope_s[...] = t
    f_copies = scatter(4, f_send, f_recv, lambda at: dot(hid_s[at], wd[...]))
    gate = gate_s[...]
    t = slope_s[...]
    slope = 0.5 * (1.0 + t) + 0.5 * c0 * gate * (1.0 - t * t) * (1.0 + 3 * 0.044715 * gate * gate)
    slope_s[...] = slope * up_s[...]
    n_f, i_f = stats(total(f_copies, f_recv))
    out = mid + n_f * g_pf[...]

    @pl.when(sec == 0)
    def _():
        sbuf[...] = out
        cross.start()
        cross.wait_recv()
        hbuf[...] = xbuf[...]

    @pl.when(sec == 1)
    def _():
        sect_out[0] = out
        hbuf[...] = x_ref[...] * valid_ref[...]

    up_g = hbuf[...]
    df, dg_pf = norm_back(n_f, i_f, g_pf[...], up_g)
    df_all[mine] = df.astype(BF16)
    arrived(spread(5, df_all, mine))
    dhid = dot_nt(df_all[...], wd[...])
    dgate_s[...] = (dhid * slope_s[...]).astype(BF16)
    dup_s[...] = (dhid * act_s[...]).astype(BF16)
    db_copies = scatter(
        6, db_send, db_recv,
        lambda at: dot_nt(dgate_s[at], wg[...]) + dot_nt(dup_s[at], wu[...]),
    )
    dwd[0] = dot_tn(hid_s[...], df_all[...])
    advance(0, 0)
    dwg[0] = dot_tn(b_all[...], dgate_s[...])
    advance(0, 1)
    dwu[0] = dot_tn(b_all[...], dup_s[...])
    advance(0, 2)
    db = total(db_copies, db_recv)
    mid_back, dg_ff = norm_back(n_mid, i_mid, g_ff[...], db)
    dmid = hbuf[...] + mid_back
    dmid_s[...] = dmid
    do, dg_pa = norm_back(n_o, i_o, g_pa[...], dmid)
    do_all[mine] = do.astype(BF16)
    do_copies = spread(7, do_all, mine)
    arrived(do_copies)
    datt_f = dot_nt(do_all[...], wo[...])
    datt = datt_f.astype(BF16)
    delta = jnp.sum(datt.astype(F32) * att_s[...].astype(F32), axis=-1, keepdims=True)
    p = p_s[...]
    ds = (p * (dot_nt(datt, v_s[...]) - delta)).astype(BF16)
    dqr = dot(ds, kr_s[...]) * scale
    dkr = dot_tn(ds, qr_s[...]) * scale
    dv = dot_tn(p.astype(BF16), datt)
    dq, dg_q = norm_back(qn_s[...], qi_s[...], g_q[...], rotate_back(dqr, cos, sin))
    dk, dg_k = norm_back(kn_s[...], ki_s[...], g_k[...], rotate_back(dkr, cos, sin))
    dq_s[...] = dq.astype(BF16)
    dk_s[...] = dk.astype(BF16)
    dv_s[...] = dv.astype(BF16)
    da_copies = scatter(
        8, da_send, da_recv,
        lambda at: dot_nt(dq_s[at], wq[...]) + dot(dk_s[at], wkf[...]) + dot(dv_s[at], wvf[...]),
    )
    for j in range(tp):
        kv_send[j] = jnp.concatenate(
            [dk_s[:, j * cols:(j + 1) * cols], dv_s[:, j * cols:(j + 1) * cols]], axis=1
        )
    kv_copies = []
    for k in range(1, tp):
        c = copy(9, k, kv_send.at[peers[k]], kv_recv.at[k - 1])
        c.start()
        kv_copies.append(c)
    pending.extend(kv_copies)
    dwo[0] = dot_tn(att_s[...], do_all[...])
    advance(0, 3)
    da = total(da_copies, da_recv)
    in_back, dg_attn = norm_back(n_in, i_in, g_attn[...], da)
    dh = dmid_s[...] + in_back

    @pl.when(sec == 1)
    def _():
        sbuf[...] = dh
        cross.start()

    @pl.when(sec == 0)
    def _():
        sect_out[0] = dh

    zero = jnp.zeros((1, width - dg_q.shape[1] - dg_k.shape[1]), F32)
    gains = jnp.concatenate(
        [dg_attn, dg_pa, dg_ff, dg_pf, jnp.concatenate([dg_q, dg_k, zero], axis=1),
         jnp.zeros((3, width), F32)], axis=0
    )
    gain_copies = []
    if inside:
        gain_tp[me] = gains
        for k in range(1, tp):
            c = pltpu.make_async_remote_copy(
                src_ref=gain_tp.at[me], dst_ref=gain_tp.at[me], send_sem=g_send.at[0, k - 1],
                recv_sem=g_recv.at[0, k - 1], device_id={"tp": peers[k]}, device_id_type=MESH,
            )
            c.start()
            gain_copies.append(c)
    else:
        gains_out[...] = gains
    dwq[0] = dot_tn(a_all[...], dq_s[...])
    advance(0, 4)
    dkv = kv_send[me].astype(F32)
    for k in range(1, tp):
        kv_copies[k - 1].wait_recv()
        dkv = dkv + kv_recv[k - 1].astype(F32)
    dkv_s[...] = dot_tn(dkv.astype(BF16), a_all[...])
    advance(0, 5)
    if inside:
        advance(1, 0, 1)
        advance(2, 0)
        advance(1, 2)
        advance(2, 1)
        for c in gain_copies:
            c.wait_recv()
        gain_dp[z] = sum(gain_tp[j] for j in range(tp))
        more = []
        for k in range(1, dp):
            c = pltpu.make_async_remote_copy(
                src_ref=gain_dp.at[z], dst_ref=gain_dp.at[z], send_sem=g_send.at[1, k - 1],
                recv_sem=g_recv.at[1, k - 1], device_id={"dp": lax.rem(z + k, dp)},
                device_id_type=MESH,
            )
            c.start()
            more.append(c)
        pending.extend(gain_copies + more)
        advance(3, 0)
        advance(2, 2)
        advance(1, 3)
        advance(3, 1)
        advance(2, 3)
        advance(1, 4)
        advance(3, 2)
        advance(2, 4)
        advance(1, 5)
        advance(3, 3)
        advance(2, 5)
        advance(3, 4)
        advance(3, 5)
        for c in more:
            c.wait_recv()
        gains_out[...] = sum(gain_dp[j] for j in range(dp))
        advance(4, 0, 1, 2, 3, 4, 5)
    else:
        owk[0] = dkv_s[:cols].astype(BF16)
        owv[0] = dkv_s[cols:].astype(BF16)
        for final, grad in ((owq, dwq), (owo, dwo), (owg, dwg), (owu, dwu), (owd, dwd)):
            final[...] = grad[...].astype(BF16)
    for c in pending:
        c.wait_send()
    cross.wait_send()
    if inside:
        @pl.when(edge)
        def _():
            for c in plan:
                c[0].wait_send()

        @pl.when(middle)
        def _():
            for c in plan:
                for step in (1, 2, 3):
                    c[step].wait_send()


def finish_kernel(hd, sect, gains, *refs):
    mats, out, outs = refs[:7], refs[7], refs[8:]
    out[...] = sect[...]
    for i in range(4):
        outs[i][...] = gains[i:i + 1]
    outs[4][...] = gains[4:5, :hd]
    outs[5][...] = gains[4:5, hd:2 * hd]
    for m, o in zip(mats, outs[6:]):
        o[...] = m[...].astype(F32)


def local(
    section_in, seq_lengths, attn_norm, q_norm, k_norm, w_query, w_key, w_value, w_out,
    post_attn_norm, ff_norm, w_gate, w_up, w_down, post_ff_norm,
):
    first = lax.axis_index("section") == 0
    tp = lax.axis_size("tp")
    tp_index = lax.axis_index("tp")
    x = section_in[0]
    rows, width = x.shape
    n = rows * tp
    hd = q_norm.shape[-1]
    ff = w_gate.shape[2]
    cols = w_key.shape[2]
    segment, position, valid_rows = layout(seq_lengths, n)
    valid = lax.dynamic_slice_in_dim(valid_rows, tp_index * rows, rows, 0).astype(F32)[:, None]
    window = jnp.where(first, WINDOW, n + 1)
    rope_base = jnp.where(first, 10000.0, 1000000.0).astype(F32)
    cos, sin = tables(position, rope_base, hd)
    distance = position[:, None] - position[None, :]
    visible = (segment[:, None] == segment[None, :]) & (distance >= 0) & (distance < window)
    bias = jnp.where(visible, 0.0, -1e30).astype(F32)
    dp = lax.axis_size("dp")
    inside = dp == 4 and width % 64 == 0 and hd % 64 == 0 and ff % 64 == 0
    sds = jax.ShapeDtypeStruct
    vm = pltpu.VMEM
    rs = lambda: vm((tp - 1, rows, width), BF16)
    ag = lambda: vm((n, width), BF16)
    across = [vm((2 * cols, width), F32)]
    if inside:
        across = []
        for m, w in ((ff, width), (width, ff), (width, ff), (hd, width), (width, hd), (2 * cols, width)):
            across += [vm((m, w), BF16)] * 2 + [vm((m // 2, w), BF16)] * 2 + [vm((m, w), BF16)]
        sem = pltpu.SemaphoreType.DMA
        across += [
            vm((2 * cols, width), F32), vm((tp, 8, width), F32), vm((dp, 8, width), F32),
            sem((6, 4)), sem((6, 4)), sem((2, max(tp, dp) - 1)), sem((2, max(tp, dp) - 1)),
        ]
    shapes = [
        (1, width, hd), (1, cols, width), (1, cols, width), (1, hd, width), (1, width, ff),
        (1, width, ff), (1, ff, width),
    ]
    outs = pl.pallas_call(
        functools.partial(layer_kernel, tp, dp, inside),
        out_shape=[
            sds((1, rows, width), F32), sds((8, width), F32),
        ] + [sds(shape, BF16) for shape in shapes],
        in_specs=[pl.BlockSpec(memory_space=pltpu.VMEM)] * 18,
        out_specs=[pl.BlockSpec(memory_space=pltpu.VMEM)] * 9,
        scratch_shapes=[vm(shapes[i], F32) for i in (0, 3, 4, 5, 6)] + [
            vm((hd, width), BF16), vm((hd, width), BF16),
            vm((rows, width), F32), vm((rows, width), F32), vm((rows, width), F32),
            ag(), ag(), ag(), ag(),
            rs(), rs(), rs(), rs(), rs(), rs(), rs(), rs(),
            vm((tp, n, 2 * cols), BF16), vm((tp - 1, n, 2 * cols), BF16),
            vm((n, hd), F32), vm((n, 1), F32), vm((n, hd), F32), vm((n, 1), F32),
            vm((n, hd), BF16), vm((n, hd), BF16), vm((n, hd), BF16), vm((n, n), F32), vm((n, hd), BF16),
            vm((n, ff), F32), vm((n, ff), F32), vm((n, ff), F32), vm((n, ff), BF16), vm((n, ff), F32),
            vm((n, ff), BF16), vm((n, ff), BF16), vm((n, hd), BF16), vm((n, hd), BF16), vm((n, hd), BF16),
            vm((rows, width), F32), vm((rows, width), F32),
            pltpu.SemaphoreType.DMA((11, tp - 1)), pltpu.SemaphoreType.DMA((11, tp - 1)),
            pltpu.SemaphoreType.DMA, pltpu.SemaphoreType.DMA,
        ] + across,
        compiler_params=pltpu.CompilerParams(
            collective_id=0, has_side_effects=True, vmem_limit_bytes=56 * 1024 * 1024
        ),
    )(
        x, valid, bias, cos, sin, attn_norm, q_norm, k_norm, w_query[0], w_key[0].T, w_value[0].T,
        w_out[0], post_attn_norm, ff_norm, w_gate[0], w_up[0], w_down[0], post_ff_norm,
    )
    section_out, gains = outs[0], outs[1]
    mats = outs[2:]
    if not inside:
        gains = lax.psum(gains, ("dp", "tp"))
        mats = lax.psum(tuple(mats), "dp")
    ends = pl.pallas_call(
        functools.partial(finish_kernel, hd),
        out_shape=[sds((1, rows, width), F32)] + [sds((1, width), F32)] * 4 + [sds((1, hd), F32)] * 2
        + [sds(shape, F32) for shape in shapes],
        in_specs=[pl.BlockSpec(memory_space=pltpu.VMEM)] * 9,
        out_specs=[pl.BlockSpec(memory_space=pltpu.VMEM)] * 14,
        compiler_params=pltpu.CompilerParams(vmem_limit_bytes=32 * 1024 * 1024),
    )(section_out, gains, *mats)
    g_attn, g_pa, g_ff, g_pf, g_q, g_k, wq, wk, wv, wo, wg, wu, wd = ends[1:]
    return (
        ends[0], g_attn, g_q, g_k, wq, jnp.swapaxes(wk, 1, 2), jnp.swapaxes(wv, 1, 2), wo, g_pa,
        g_ff, wg, wu, wd, g_pf,
    )


def solution(mesh):
    grid = P("section", None, "tp")
    down = P("section", "tp", None)
    gain = P("section", None)
    act = P("section", ("dp", "tp"), None)
    return jax.shard_map(
        local,
        mesh=mesh,
        in_specs=(
            act, P("dp"), gain, gain, gain, grid, grid, grid, down, gain, gain, grid, grid, down, gain,
        ),
        out_specs=(
            act, gain, gain, gain, grid, grid, grid, down, gain, gain, grid, grid, down, gain,
        ),
        check_vma=False,
    )
```
